1024 devices in a mesh: dp: 64 (over z, core), tensor: 16 (over x, y).
Axes of the slice: x: 4, y: 4, z: 32, core: 2. Of those that a mesh axis runs over, the one named last changes fastest.
Arguments:
- activations: bfloat16 [49152, 4096], P('dp', 'tensor'), may hold values from -0.21875 to 0.21875
- out_grads: bfloat16 [49152, 4096], P('dp'), may hold values from -6 to 6
- error_memory: bfloat16 [64, 4096, 4096], P('dp', 'tensor'), may hold values from -6 to 6
- q_init: float32 [4096, 64], replicated, may hold values from -0.09375 to 0.09375
Outputs:
- p_basis: float32 [4096, 64], P('tensor')
- q_factor: float32 [4096, 64], replicated
The draws below stay inside these ranges and needn't reach their ends.
All inputs are finite; a program needn't handle non-finite values.
Results may differ from the reference program's by a relative error of at most 0.0003.
Values sent between devices are 32-bit elements; how exact they have to be, the bound alone decides.
A program may use at most 64 MiB of HBM per device.

```python
import jax
import jax.numpy as jnp
from jax import lax

HID = 4096
DW = 4096
RANK = 64
TOK = 768
TOKENS = 49152
REPLICAS = 64
N_DP = 64


def shard_levels(stream_key, dims, split, least, top_value):
    gain = 1.0
    for dim, parts in split:
        heights = jax.random.uniform(jax.random.fold_in(jax.random.fold_in(stream_key, 6), dim), (parts,), jnp.float32, least / len(split), top_value / len(split))
        gain = gain * jnp.repeat(jnp.exp(heights), dims[dim] // parts).reshape((-1,) + (1,) * (len(dims) - 1 - dim))
    return gain


def noise(rng, shape, scale, most, shards=(), dtype=jnp.bfloat16):
    level = shard_levels(rng, shape, shards, -0.22, 0.18) if shards else 1.0
    entries = jax.random.normal(rng, shape, jnp.float32) * scale * level
    return jnp.minimum(jnp.maximum(entries, -most), most).astype(dtype)


def setup_inputs(seed: int = 0) -> dict:
    keys = jax.random.split(jax.random.key(seed), 5)
    activations = noise(keys[0], (TOKENS, HID), TOK ** -0.5, 0.21875, ((0, 64), (1, 16)))
    out_grads = noise(keys[1], (TOKENS, DW), 1.0, 6.0, ((0, 64),))
    error_memory = noise(keys[2], (REPLICAS, HID, DW), 1.0, 6.0, ((0, 64), (1, 16)))
    q_init = noise(keys[3], (DW, RANK), DW ** -0.5, 0.09375, (), jnp.float32)
    return dict(activations=activations, out_grads=out_grads, error_memory=error_memory, q_init=q_init)


def reference(activations, out_grads, error_memory, q_init):
    highest = lax.Precision.HIGHEST
    inputs = activations.reshape(N_DP, TOK, HID)
    grads = out_grads.reshape(N_DP, TOK, DW)

    def left_step(total, items):
        act, grd, err = items
        act = act.astype(jnp.float32)
        grd = grd.astype(jnp.float32)
        err = err.astype(jnp.float32)
        term = jnp.dot(act.T, jnp.dot(grd, q_init, precision=highest), precision=highest)
        term = term + jnp.dot(err, q_init, precision=highest)
        return (total + term, None)
    p_sum, unused = lax.scan(left_step, jnp.zeros((HID, RANK), jnp.float32), (inputs, grads, error_memory))
    gram = jnp.dot(p_sum.T, p_sum, precision=highest)
    lower = jnp.linalg.cholesky(gram)
    p_orth = lax.linalg.triangular_solve(lower, p_sum, left_side=False, lower=True, transpose_a=True)

    def right_step(total, items):
        act, grd, err = items
        act = act.astype(jnp.float32)
        grd = grd.astype(jnp.float32)
        err = err.astype(jnp.float32)
        term = jnp.dot(grd.T, jnp.dot(act, p_orth, precision=highest), precision=highest)
        term = term + jnp.dot(err.T, p_orth, precision=highest)
        return (total + term, None)
    q_total, unused = lax.scan(right_step, jnp.zeros((DW, RANK), jnp.float32), (inputs, grads, error_memory))
    return (p_orth * jnp.sqrt(jnp.float32(HID)), q_total / N_DP)
```

```python
import jax
import jax.numpy as jnp
from jax import lax
from jax.experimental import pallas as pl
from jax.experimental.pallas import tpu as pltpu
from jax.sharding import PartitionSpec as P

MESH = pl.DeviceIdType.MESH
F32 = jnp.float32
BF16 = jnp.bfloat16
HIGHEST = lax.Precision.HIGHEST
NZ = 32
NT = 16
RANK = 64
LANES = 128
WIN = 8
GROUPS = NZ // WIN
LEFT, RIGHT = -(WIN // 2 - 1), WIN // 2
NN = (((1,), (0,)), ((), ()))
NT_DIMS = (((1,), (1,)), ((), ()))


def dot(a, b, dims=NN, precision=None):
    return lax.dot_general(a, b, dims, precision=precision, preferred_element_type=F32)


def split3(v):
    hi = v.astype(BF16)
    rest = v - hi.astype(F32)
    mid = rest.astype(BF16)
    low = (rest - mid.astype(F32)).astype(BF16)
    return jnp.concatenate([hi, mid, low], axis=0)


def fold3(v):
    return v[:RANK] + (v[RANK:2 * RANK] + v[2 * RANK:])


def wait(sem, ref):
    pltpu.make_async_copy(ref, ref, sem).wait()


def invert_factor(gram):
    row = lax.broadcasted_iota(jnp.int32, (RANK, 2 * RANK), 0)
    lane = lax.broadcasted_iota(jnp.int32, (RANK, 2 * RANK), 1)
    m = jnp.where(lane < RANK, gram, jnp.where(lane - RANK == row, 1.0, 0.0))
    scale = jnp.zeros((RANK, 2 * RANK), F32)
    for k in range(RANK):
        col = jnp.broadcast_to(m[:, k:k + 1], m.shape)
        pivot = col[k:k + 1, :]
        scaled = m[k:k + 1, :] / pivot
        scale = jnp.where(row == k, pivot, scale)
        m = m - jnp.where(row > k, col, 0.0) * scaled
    m = m * lax.rsqrt(scale)
    return m[:, RANK:]


def kernel(act_hbm, grd_hbm, err_hbm, q0_hbm, pb_ref, out_ref,
           x, act, q0, q3, w3, p_src, p_rs, p_far, p_red, p_all,
           g_src, g_rs, g_own, g_all,
           q_loc, q_d, q_s, q_x, z_src, z_rs, z_far, z_red, z_all,
           load_sem, send_sem, recv_sem, piece_sem):
    dp = lax.axis_index("dp")
    t = lax.axis_index("tensor")
    z = dp // 2
    core = dp % 2
    other = 1 - core
    place = z % WIN
    group = z // WIN

    def at(zz, cc):
        return ((zz + NZ) % NZ) * 2 + cc

    def send(src, dst, phase, dev, recv=None):
        pltpu.make_async_remote_copy(
            src_ref=src, dst_ref=dst, send_sem=send_sem.at[phase],
            recv_sem=recv_sem.at[phase] if recv is None else recv,
            device_id=dev, device_id_type=MESH).start()

    def tile(i):
        return pl.ds(pl.multiple_of(i * 8, 8), 8)

    copies = [pltpu.make_async_copy(q0_hbm, q0, load_sem.at[0])]
    copies.append(pltpu.make_async_copy(err_hbm, x.at[pl.ds(768, 256)], load_sem.at[1]))
    for r in range(3):
        copies.append(pltpu.make_async_copy(
            grd_hbm.at[pl.ds(256 * r, 256)], x.at[pl.ds(256 * r, 256)], load_sem.at[2 + r]))
    copies.append(pltpu.make_async_copy(act_hbm, act, load_sem.at[5]))
    for c in copies:
        c.start()

    barrier = pltpu.get_barrier_semaphore()
    near = [(d, c) for d in range(-WIN // 2, WIN // 2 + 1) for c in (0, 1)]
    for d, c in near:
        cc = core if c == 0 else other
        if (d, c) != (0, 0):
            pl.semaphore_signal(barrier, inc=1, device_id=(at(z + d, cc), t), device_id_type=MESH)
    for d in (-WIN, WIN):
        pl.semaphore_signal(barrier, inc=1, device_id=(at(z + d, core), t), device_id_type=MESH)
    for k in range(1, NT):
        pl.semaphore_signal(barrier, inc=1, device_id=(dp, t ^ k), device_id_type=MESH)

    copies[0].wait()
    q3[...] = split3(q0[...])
    copies[1].wait()
    left = fold3(dot(q3[...], x[768:1024, :], NT_DIMS))
    copies[5].wait()
    acc = None
    for r in range(3):
        copies[2 + r].wait()
        y = fold3(dot(q3[...], x[256 * r:256 * (r + 1), :], NT_DIMS))
        term = dot(split3(y), act[256 * r:256 * (r + 1), :])
        acc = term if acc is None else acc + term
    p_src[...] = fold3(acc) + left
    pl.semaphore_wait(barrier, 2 * (WIN + 1) - 1 + 2 + NT - 1)

    slot = 0
    for d in range(LEFT, RIGHT + 1):
        e = -d
        for same in (0, 1):
            if d == 0 and same == 1:
                continue
            cc = core if same else other
            piece = (z + e + NZ) % WIN
            send(p_src.at[tile(piece), pl.ds(pl.multiple_of(cc * LANES, LANES), LANES)],
                 p_rs.at[slot], 0, (at(z + e, cc), t))
            slot += 1
    own = p_src[tile(place), pl.ds(pl.multiple_of(core * LANES, LANES), LANES)]
    wait(recv_sem.at[0], p_rs)
    total = own
    for s in range(2 * WIN - 1):
        total = total + p_rs[s]
    p_far[group] = total
    send(p_far.at[group], p_far.at[group], 1, (at(z - WIN, core), t))
    send(p_far.at[group], p_far.at[group], 1, (at(z + WIN, core), t))
    wait(recv_sem.at[1], p_rs.at[pl.ds(0, 2)])
    step = 1 - 2 * core
    relay = (group + step + GROUPS) % GROUPS
    send(p_far.at[relay], p_far.at[relay], 2, (at(z - step * WIN, core), t))
    wait(recv_sem.at[2], p_rs.at[0])
    total = (p_far[0] + p_far[1]) + (p_far[2] + p_far[3])
    p_red[...] = total
    rows, cols = tile(place), pl.ds(pl.multiple_of(core * LANES, LANES), LANES)
    p_all[rows, cols] = total
    for d in range(LEFT, RIGHT + 1):
        for same in (0, 1):
            if d == 0 and same == 1:
                continue
            send(p_red, p_all.at[rows, cols], 3, (at(z + d, core if same else other), t))
    wait(recv_sem.at[3], p_rs)

    p_sum = p_all[...]
    gram = dot(p_sum, jnp.concatenate([p_sum, p_sum], axis=0), NT_DIMS, HIGHEST)
    for i in range(NT):
        g_src[i, 0:4, :] = gram[4 * i:4 * i + 4]
        g_src[i, 4:8, :] = gram[4 * i:4 * i + 4]
    for k in range(1, NT):
        send(g_src.at[t ^ k], g_rs.at[k - 1], 4, (dp, t ^ k))

    p3 = split3(p_sum)
    w3[:, 768:1024] = p3
    w3[:, 0:768] = split3(fold3(dot(p3, act[...], NT_DIMS)))

    def chunk(k):
        j = t ^ k
        v = fold3(dot(w3[...], x[:, pl.ds(pl.multiple_of(j * 256, 256), 256)]))
        q_loc[k, 0] = v[:, :LANES]
        q_loc[k, 1] = v[:, LANES:]
        send(q_loc.at[k, other], q_d.at[k], 5, (dp + other - core, t), piece_sem.at[k])

    def forward(k):
        wait(piece_sem.at[k], q_d.at[k])
        q_s[k] = q_loc[k, core] + q_d[k]
        if k > 0:
            send(q_s.at[k], q_x.at[k - 1], 6, (dp, t ^ k))

    order = list(range(1, NT)) + [0]
    lag = 6
    for i in range(NT + lag):
        if i < NT:
            chunk(order[i])
        if i >= lag:
            forward(order[i - lag])

    wait(recv_sem.at[4], g_rs)
    total = g_src[t]
    for k in range(NT - 1):
        total = total + g_rs[k]
    g_own[...] = total
    g_all[t] = total
    for k in range(1, NT):
        send(g_own, g_all.at[t], 7, (dp, t ^ k))

    wait(recv_sem.at[6], q_x)
    total = q_s[0]
    for k in range(NT - 1):
        total = total + q_x[k]
    z_src[...] = total

    slot = 0
    for d in range(LEFT, RIGHT + 1):
        if d != 0:
            piece = (z - d + NZ) % WIN
            send(z_src.at[tile(piece)], z_rs.at[slot], 8, (at(z - d, core), t))
            slot += 1
    own = z_src[tile(place)]
    wait(recv_sem.at[8], z_rs)
    total = own
    for s in range(WIN - 1):
        total = total + z_rs[s]
    z_far[group] = total
    for m in range(1, GROUPS):
        send(z_far.at[group], z_far.at[group], 9, (at(z + m * WIN, core), t))

    wait(recv_sem.at[7], g_rs)
    inverse = invert_factor(jnp.concatenate([g_all[i, 0:4, :] for i in range(NT)], axis=0))
    pb_ref[...] = dot(inverse, p_sum, NN, HIGHEST) * 64.0

    wait(recv_sem.at[9], z_rs.at[pl.ds(0, GROUPS - 1)])
    total = (z_far[0] + z_far[1]) + (z_far[2] + z_far[3])
    z_red[...] = total
    z_all[rows, :] = total
    for d in range(LEFT, RIGHT + 1):
        if d != 0:
            send(z_red, z_all.at[rows], 10, (at(z + d, core), t))
    wait(recv_sem.at[10], z_rs)

    def columns(tt, cc):
        return pl.ds(pl.multiple_of((tt * 2 + cc) * LANES, LANES), LANES)

    mine = columns(t, core)
    out_ref[:, mine] = dot(inverse, z_all[...], NN, HIGHEST) * (1.0 / 64.0)
    for k in range(1, NT):
        send(out_ref.at[:, mine], out_ref.at[:, mine], 11, (dp, t ^ k), piece_sem.at[NT + k])
    sibling = (dp + other - core, t)
    send(out_ref.at[:, mine], out_ref.at[:, mine], 12, sibling)
    for k in range(1, NT):
        got = columns(t ^ k, core)
        wait(piece_sem.at[NT + k], out_ref.at[:, got])
        send(out_ref.at[:, got], out_ref.at[:, got], 12, sibling)
    wait(recv_sem.at[12], q_d)

    wait(send_sem.at[0], p_rs)
    wait(send_sem.at[1], p_rs.at[pl.ds(0, 2)])
    wait(send_sem.at[2], p_rs.at[0])
    wait(send_sem.at[3], p_rs)
    wait(send_sem.at[4], g_rs)
    wait(send_sem.at[5], q_d)
    wait(send_sem.at[6], q_x)
    wait(send_sem.at[7], g_rs)
    wait(send_sem.at[8], z_rs)
    wait(send_sem.at[9], z_rs.at[pl.ds(0, GROUPS - 1)])
    wait(send_sem.at[10], z_rs)
    wait(send_sem.at[11], q_x)
    wait(send_sem.at[12], q_d)


def local(activations, out_grads, error_memory, q_init):
    any_spec = pl.BlockSpec(memory_space=pl.ANY)
    vmem = pl.BlockSpec(memory_space=pltpu.VMEM)
    piece = (RANK, LANES)
    scratch = [
        pltpu.VMEM((1024, 4096), BF16),
        pltpu.VMEM((768, 256), BF16),
        pltpu.VMEM((RANK, 4096), F32),
        pltpu.VMEM((3 * RANK, 4096), BF16),
        pltpu.VMEM((3 * RANK, 1024), BF16),
        pltpu.VMEM((RANK, 256), F32),
        pltpu.VMEM((2 * WIN - 1, 8, LANES), F32),
        pltpu.VMEM((GROUPS, 8, LANES), F32),
        pltpu.VMEM((8, LANES), F32),
        pltpu.VMEM((RANK, 256), F32),
        pltpu.VMEM((NT, 8, LANES), F32),
        pltpu.VMEM((NT - 1, 8, LANES), F32),
        pltpu.VMEM((8, LANES), F32),
        pltpu.VMEM((NT, 8, LANES), F32),
        pltpu.VMEM((NT, 2) + piece, F32),
        pltpu.VMEM((NT,) + piece, F32),
        pltpu.VMEM((NT,) + piece, F32),
        pltpu.VMEM((NT - 1,) + piece, F32),
        pltpu.VMEM(piece, F32),
        pltpu.VMEM((WIN - 1, 8, LANES), F32),
        pltpu.VMEM((GROUPS, 8, LANES), F32),
        pltpu.VMEM((8, LANES), F32),
        pltpu.VMEM(piece, F32),
        pltpu.SemaphoreType.DMA((6,)),
        pltpu.SemaphoreType.DMA((13,)),
        pltpu.SemaphoreType.DMA((13,)),
        pltpu.SemaphoreType.DMA((2 * NT,)),
    ]
    basis, right = pl.pallas_call(
        kernel,
        name="powersgd",
        out_shape=(
            jax.ShapeDtypeStruct((RANK, 256), F32),
            jax.ShapeDtypeStruct((RANK, 4096), F32),
        ),
        in_specs=[any_spec] * 4,
        out_specs=(vmem, vmem),
        scratch_shapes=scratch,
        compiler_params=pltpu.CompilerParams(
            collective_id=0, has_side_effects=True, vmem_limit_bytes=60 * 2**20),
    )(activations, out_grads, error_memory[0], q_init.T)
    return basis.T, right.T


def solution(mesh):
    return jax.shard_map(
        local,
        mesh=mesh,
        in_specs=(P("dp", "tensor"), P("dp", None), P("dp", "tensor", None), P()),
        out_specs=(P("tensor", None), P()),
        check_vma=False,
    )
```

```python
import jax
import jax.numpy as jnp
from jax import lax
from jax.experimental import pallas as pl
from jax.experimental.pallas import tpu as pltpu
from jax.sharding import PartitionSpec as P

MESH = pl.DeviceIdType.MESH
F32 = jnp.float32
BF16 = jnp.bfloat16
HIGHEST = lax.Precision.HIGHEST
NZ = 32
NT = 16
RANK = 64
LANES = 128
WIN = 4
ROWS = RANK // WIN
GROUPS = NZ // WIN
FAR_ORDER = sorted(range(1, GROUPS), key=lambda m: -min(m, GROUPS - m))
LEFT, RIGHT = -(WIN // 2 - 1), WIN // 2
ORDER = (10, 11, 14, 9, 6, 15, 5, 7, 13, 2, 8, 1, 4, 3, 12, 0)
BATCH = 4
NN = (((1,), (0,)), ((), ()))
NT_DIMS = (((1,), (1,)), ((), ()))


def dot(a, b, dims=NN, precision=None):
    return lax.dot_general(a, b, dims, precision=precision, preferred_element_type=F32)


def split3(v):
    hi = v.astype(BF16)
    rest = v - hi.astype(F32)
    mid = rest.astype(BF16)
    low = (rest - mid.astype(F32)).astype(BF16)
    return jnp.concatenate([hi, mid, low], axis=0)


def fold3(v):
    return v[:RANK] + (v[RANK:2 * RANK] + v[2 * RANK:])


def wait(sem, ref):
    pltpu.make_async_copy(ref, ref, sem).wait()


def invert_factor(gram):
    row = lax.broadcasted_iota(jnp.int32, (RANK, 2 * RANK), 0)
    lane = lax.broadcasted_iota(jnp.int32, (RANK, 2 * RANK), 1)
    m = jnp.where(lane < RANK, gram, jnp.where(lane - RANK == row, 1.0, 0.0))
    scale = jnp.zeros((RANK, 2 * RANK), F32)
    for k in range(RANK):
        col = jnp.broadcast_to(m[:, k:k + 1], m.shape)
        pivot = col[k:k + 1, :]
        scaled = m[k:k + 1, :] / pivot
        scale = jnp.where(row == k, pivot, scale)
        m = m - jnp.where(row > k, col, 0.0) * scaled
    m = m * lax.rsqrt(scale)
    return m[:, RANK:]


def kernel(act_hbm, grd_hbm, err_hbm, q0_hbm, pb_ref, out_ref,
           x, act, q0, q3, w3, p_src, p_rs, p_far, p_red, p_all,
           g_src, g_rs, g_own, g_all,
           q_loc, q_d, q_s, q_x, z_src, z_rs, z_far, z_red, z_all,
           load_sem, send_sem, recv_sem, piece_sem, relay_sem):
    dp = lax.axis_index("dp")
    t = lax.axis_index("tensor")
    z = dp // 2
    core = dp % 2
    other = 1 - core
    sibling = (dp + other - core, t)
    place = z % WIN
    group = z // WIN

    def at(zz, cc):
        return ((zz + NZ) % NZ) * 2 + cc

    def send(src, dst, phase, dev, recv=None):
        pltpu.make_async_remote_copy(
            src_ref=src, dst_ref=dst, send_sem=send_sem.at[phase],
            recv_sem=recv_sem.at[phase] if recv is None else recv,
            device_id=dev, device_id_type=MESH).start()

    def tile(i):
        return pl.ds(pl.multiple_of(i * ROWS, ROWS), ROWS)

    copies = [pltpu.make_async_copy(q0_hbm, q0, load_sem.at[0])]
    copies.append(pltpu.make_async_copy(err_hbm, x.at[pl.ds(768, 256)], load_sem.at[1]))
    for r in range(3):
        copies.append(pltpu.make_async_copy(
            grd_hbm.at[pl.ds(256 * r, 256)], x.at[pl.ds(256 * r, 256)], load_sem.at[2 + r]))
    copies.append(pltpu.make_async_copy(act_hbm, act, load_sem.at[5]))
    for c in copies:
        c.start()

    barrier = pltpu.get_barrier_semaphore()
    near = [(d, c) for d in range(-WIN // 2, WIN // 2 + 1) for c in (0, 1)]
    for d, c in near:
        cc = core if c == 0 else other
        if (d, c) != (0, 0):
            pl.semaphore_signal(barrier, inc=1, device_id=(at(z + d, cc), t), device_id_type=MESH)
    far = [d for d in (-8, 8, -4, 4) if abs(d) > WIN // 2]
    for d in far:
        pl.semaphore_signal(barrier, inc=1, device_id=(at(z + d, core), t), device_id_type=MESH)
    for k in range(1, NT):
        pl.semaphore_signal(barrier, inc=1, device_id=(dp, t ^ k), device_id_type=MESH)

    copies[0].wait()
    q3[...] = split3(q0[...])
    copies[1].wait()
    left = fold3(dot(q3[...], x[768:1024, :], NT_DIMS))
    copies[5].wait()
    acc = None
    for r in range(3):
        copies[2 + r].wait()
        y = fold3(dot(q3[...], x[256 * r:256 * (r + 1), :], NT_DIMS))
        term = dot(split3(y), act[256 * r:256 * (r + 1), :])
        acc = term if acc is None else acc + term
    p_src[...] = fold3(acc) + left
    pl.semaphore_wait(barrier, len(near) - 1 + len(far) + NT - 1)
    for d in (-8, 8):
        pl.semaphore_signal(relay_sem, inc=1, device_id=(at(z + d, core), t), device_id_type=MESH)

    slot = 0
    for d in range(LEFT, RIGHT + 1):
        e = -d
        for same in (0, 1):
            if d == 0 and same == 1:
                continue
            cc = core if same else other
            piece = (z + e + NZ) % WIN
            send(p_src.at[tile(piece), pl.ds(pl.multiple_of(cc * LANES, LANES), LANES)],
                 p_rs.at[slot], 0, (at(z + e, cc), t))
            slot += 1
    own = p_src[tile(place), pl.ds(pl.multiple_of(core * LANES, LANES), LANES)]
    wait(recv_sem.at[0], p_rs)
    total = own
    for s in range(2 * WIN - 1):
        total = total + p_rs[s]
    p_far[group] = total
    pl.semaphore_wait(relay_sem, 2)
    for m in FAR_ORDER:
        send(p_far.at[group], p_far.at[group], 1, (at(z + m * WIN, core), t))
    wait(recv_sem.at[1], p_far.at[pl.ds(0, GROUPS - 1)])
    total = p_far[0]
    for m in range(1, GROUPS):
        total = total + p_far[m]
    p_red[...] = total
    rows, cols = tile(place), pl.ds(pl.multiple_of(core * LANES, LANES), LANES)
    p_all[rows, cols] = total
    for d in range(LEFT, RIGHT + 1):
        for same in (0, 1):
            if d == 0 and same == 1:
                continue
            send(p_red, p_all.at[rows, cols], 3, (at(z + d, core if same else other), t))
    wait(recv_sem.at[3], p_rs)

    p_sum = p_all[...]

    p3 = split3(p_sum)
    w3[:, 768:1024] = p3
    w3[:, 0:768] = split3(fold3(dot(p3, act[...], NT_DIMS)))

    def compute(b):
        for i in range(b * BATCH, (b + 1) * BATCH):
            j = t ^ ORDER[i]
            v = fold3(dot(w3[...], x[:, pl.ds(pl.multiple_of(j * 256, 256), 256)]))
            q_loc[0, i] = v[:, :LANES]
            q_loc[1, i] = v[:, LANES:]
        part = pl.ds(b * BATCH, BATCH)
        send(q_loc.at[other, part], q_d.at[part], 5, sibling, piece_sem.at[b])

    def forward(b):
        part = pl.ds(b * BATCH, BATCH)
        wait(piece_sem.at[b], q_d.at[part])
        q_s[part] = q_loc[core, part] + q_d[part]
        for i in range(b * BATCH, min((b + 1) * BATCH, NT - 1)):
            send(q_s.at[i], q_x.at[i], 6, (dp, t ^ ORDER[i]))

    batches = NT // BATCH
    for b in range(batches + 1):
        if b < batches:
            compute(b)
        if b > 0:
            forward(b - 1)

    gram = dot(p_sum, jnp.concatenate([p_sum, p_sum], axis=0), NT_DIMS, HIGHEST)
    for i in range(NT):
        g_src[i, 0:4, :] = gram[4 * i:4 * i + 4]
        g_src[i, 4:8, :] = gram[4 * i:4 * i + 4]
    for k in range(1, NT):
        send(g_src.at[t ^ k], g_rs.at[k - 1], 4, (dp, t ^ k))

    wait(recv_sem.at[4], g_rs)
    total = g_src[t]
    for k in range(NT - 1):
        total = total + g_rs[k]
    g_own[...] = total
    g_all[t] = total
    for k in range(1, NT):
        send(g_own, g_all.at[t], 7, (dp, t ^ k))

    wait(recv_sem.at[6], q_x)
    total = q_s[NT - 1]
    for k in range(NT - 1):
        total = total + q_x[k]
    z_src[...] = total

    slot = 0
    for d in range(LEFT, RIGHT + 1):
        if d != 0:
            piece = (z - d + NZ) % WIN
            send(z_src.at[tile(piece)], z_rs.at[slot], 8, (at(z - d, core), t))
            slot += 1
    own = z_src[tile(place)]
    wait(recv_sem.at[8], z_rs)
    total = own
    for s in range(WIN - 1):
        total = total + z_rs[s]
    z_far[group] = total
    for m in FAR_ORDER:
        send(z_far.at[group], z_far.at[group], 9, (at(z + m * WIN, core), t))

    wait(recv_sem.at[7], g_rs)
    inverse = invert_factor(jnp.concatenate([g_all[i, 0:4, :] for i in range(NT)], axis=0))
    pb_ref[...] = dot(inverse, p_sum, NN, HIGHEST) * 64.0

    wait(recv_sem.at[9], z_far.at[pl.ds(0, GROUPS - 1)])
    total = z_far[0]
    for m in range(1, GROUPS):
        total = total + z_far[m]
    z_red[...] = total
    z_all[rows, :] = total
    for d in range(LEFT, RIGHT + 1):
        if d != 0:
            send(z_red, z_all.at[rows], 10, (at(z + d, core), t))
    wait(recv_sem.at[10], z_rs)

    def columns(tt, cc):
        return pl.ds(pl.multiple_of((tt * 2 + cc) * LANES, LANES), LANES)

    mine = columns(t, core)
    out_ref[:, mine] = dot(inverse, z_all[...], NN, HIGHEST) * (1.0 / 64.0)
    for i in range(NT - 1):
        send(out_ref.at[:, mine], out_ref.at[:, mine], 11, (dp, t ^ ORDER[i]), piece_sem.at[NT + i])
    send(out_ref.at[:, mine], out_ref.at[:, mine], 12, sibling)
    for i in reversed(range(NT - 1)):
        got = columns(t ^ ORDER[i], core)
        wait(piece_sem.at[NT + i], out_ref.at[:, got])
        send(out_ref.at[:, got], out_ref.at[:, got], 12, sibling)
    wait(recv_sem.at[12], q_d)

    wait(send_sem.at[0], p_rs)
    wait(send_sem.at[1], p_far.at[pl.ds(0, GROUPS - 1)])
    wait(send_sem.at[3], p_rs)
    wait(send_sem.at[4], g_rs)
    wait(send_sem.at[5], q_d)
    wait(send_sem.at[6], q_x)
    wait(send_sem.at[7], g_rs)
    wait(send_sem.at[8], z_rs)
    wait(send_sem.at[9], z_far.at[pl.ds(0, GROUPS - 1)])
    wait(send_sem.at[10], z_rs)
    wait(send_sem.at[11], q_x)
    wait(send_sem.at[12], q_d)


def store(basis, right, basis_hbm, right_hbm, sem):
    copies = [pltpu.make_async_copy(basis, basis_hbm, sem.at[4])]
    for i in range(4):
        rows = pl.ds(i * 16, 16)
        copies.append(pltpu.make_async_copy(right.at[rows], right_hbm.at[rows], sem.at[i]))
    for c in copies:
        c.start()
    for c in copies:
        c.wait()


def local(activations, out_grads, error_memory, q_init):
    any_spec = pl.BlockSpec(memory_space=pl.ANY)
    vmem = pl.BlockSpec(memory_space=pltpu.VMEM)
    piece = (RANK, LANES)
    scratch = [
        pltpu.VMEM((1024, 4096), BF16),
        pltpu.VMEM((768, 256), BF16),
        pltpu.VMEM((RANK, 4096), F32),
        pltpu.VMEM((3 * RANK, 4096), BF16),
        pltpu.VMEM((3 * RANK, 1024), BF16),
        pltpu.VMEM((RANK, 256), F32),
        pltpu.VMEM((2 * WIN - 1, ROWS, LANES), F32),
        pltpu.VMEM((GROUPS, ROWS, LANES), F32),
        pltpu.VMEM((ROWS, LANES), F32),
        pltpu.VMEM((RANK, 256), F32),
        pltpu.VMEM((NT, 8, LANES), F32),
        pltpu.VMEM((NT - 1, 8, LANES), F32),
        pltpu.VMEM((8, LANES), F32),
        pltpu.VMEM((NT, 8, LANES), F32),
        pltpu.VMEM((2, NT) + piece, F32),
        pltpu.VMEM((NT,) + piece, F32),
        pltpu.VMEM((NT,) + piece, F32),
        pltpu.VMEM((NT - 1,) + piece, F32),
        pltpu.VMEM(piece, F32),
        pltpu.VMEM((WIN - 1, ROWS, LANES), F32),
        pltpu.VMEM((GROUPS, ROWS, LANES), F32),
        pltpu.VMEM((ROWS, LANES), F32),
        pltpu.VMEM(piece, F32),
        pltpu.SemaphoreType.DMA((6,)),
        pltpu.SemaphoreType.DMA((13,)),
        pltpu.SemaphoreType.DMA((13,)),
        pltpu.SemaphoreType.DMA((2 * NT,)),
        pltpu.SemaphoreType.REGULAR,
    ]
    basis, right = pl.pallas_call(
        kernel,
        name="powersgd",
        out_shape=(pltpu.VMEM((RANK, 256), F32), pltpu.VMEM((RANK, 4096), F32)),
        in_specs=[any_spec] * 4,
        out_specs=(vmem, vmem),
        scratch_shapes=scratch,
        compiler_params=pltpu.CompilerParams(
            collective_id=0, has_side_effects=True, vmem_limit_bytes=60 * 2**20),
    )(activations, out_grads, error_memory[0], q_init.T)
    basis, right = pl.pallas_call(
        store,
        name="store",
        out_shape=(
            jax.ShapeDtypeStruct((RANK, 256), F32),
            jax.ShapeDtypeStruct((RANK, 4096), F32),
        ),
        in_specs=[vmem] * 2,
        out_specs=(any_spec, any_spec),
        scratch_shapes=[pltpu.SemaphoreType.DMA((5,))],
    )(basis, right)
    return basis.T, right.T


def solution(mesh):
    return jax.shard_map(
        local,
        mesh=mesh,
        in_specs=(P("dp", "tensor"), P("dp", None), P("dp", "tensor", None), P()),
        out_specs=(P("tensor", None), P()),
        check_vma=False,
    )
```

```python
import jax
import jax.numpy as jnp
from jax import lax
from jax.experimental import pallas as pl
from jax.experimental.pallas import tpu as pltpu
from jax.sharding import PartitionSpec as P

MESH = pl.DeviceIdType.MESH
F32 = jnp.float32
BF16 = jnp.bfloat16
HIGHEST = lax.Precision.HIGHEST
NZ = 32
NT = 16
RANK = 64
LANES = 128
WIN = 4
ROWS = RANK // WIN
GROUPS = NZ // WIN
FAR_ORDER = sorted(range(1, GROUPS), key=lambda m: -min(m, GROUPS - m))
WINDOW = sorted(range(-(WIN // 2 - 1), WIN // 2 + 1), key=lambda d: -abs(d))
ORDER = (10, 11, 14, 9, 6, 15, 5, 7, 13, 2, 8, 1, 4, 3, 12, 0)
BATCH = 4
NN = (((1,), (0,)), ((), ()))
NT_DIMS = (((1,), (1,)), ((), ()))


def dot(a, b, dims=NN, precision=None):
    return lax.dot_general(a, b, dims, precision=precision, preferred_element_type=F32)


def split3(v):
    hi = v.astype(BF16)
    rest = v - hi.astype(F32)
    mid = rest.astype(BF16)
    low = (rest - mid.astype(F32)).astype(BF16)
    return jnp.concatenate([hi, mid, low], axis=0)


def fold3(v):
    return v[:RANK] + (v[RANK:2 * RANK] + v[2 * RANK:])


def wait(sem, ref):
    pltpu.make_async_copy(ref, ref, sem).wait()


def invert_factor(gram):
    row = lax.broadcasted_iota(jnp.int32, (RANK, 2 * RANK), 0)
    lane = lax.broadcasted_iota(jnp.int32, (RANK, 2 * RANK), 1)
    m = jnp.where(lane < RANK, gram, jnp.where(lane - RANK == row, 1.0, 0.0))
    scale = jnp.zeros((RANK, 2 * RANK), F32)
    for k in range(RANK):
        col = jnp.broadcast_to(m[:, k:k + 1], m.shape)
        pivot = col[k:k + 1, :]
        scaled = m[k:k + 1, :] / pivot
        scale = jnp.where(row == k, pivot, scale)
        m = m - jnp.where(row > k, col, 0.0) * scaled
    m = m * lax.rsqrt(scale)
    return m[:, RANK:]


def kernel(act_hbm, grd_hbm, err_hbm, q0_hbm, pb_ref, out_ref,
           x, act, q0, q3, w3, p_src, p_rs, p_far, p_red, p_all,
           g_src, g_rs, g_own, g_all,
           q_loc, q_d, q_s, q_x, z_src, z_rs, z_far, z_red, z_all,
           load_sem, send_sem, recv_sem, piece_sem, relay_sem):
    dp = lax.axis_index("dp")
    t = lax.axis_index("tensor")
    z = dp // 2
    core = dp % 2
    other = 1 - core
    sibling = (dp + other - core, t)
    place = z % WIN
    group = z // WIN

    def at(zz, cc):
        return ((zz + NZ) % NZ) * 2 + cc

    def send(src, dst, phase, dev, recv=None):
        pltpu.make_async_remote_copy(
            src_ref=src, dst_ref=dst, send_sem=send_sem.at[phase],
            recv_sem=recv_sem.at[phase] if recv is None else recv,
            device_id=dev, device_id_type=MESH).start()

    def tile(i):
        return pl.ds(pl.multiple_of(i * ROWS, ROWS), ROWS)

    copies = [pltpu.make_async_copy(q0_hbm, q0, load_sem.at[0])]
    copies.append(pltpu.make_async_copy(err_hbm, x.at[pl.ds(768, 256)], load_sem.at[1]))
    for r in range(3):
        copies.append(pltpu.make_async_copy(
            grd_hbm.at[pl.ds(256 * r, 256)], x.at[pl.ds(256 * r, 256)], load_sem.at[2 + r]))
    copies.append(pltpu.make_async_copy(act_hbm, act, load_sem.at[5]))
    for c in copies:
        c.start()

    barrier = pltpu.get_barrier_semaphore()
    near = [(d, c) for d in range(-WIN // 2, WIN // 2 + 1) for c in (0, 1)]
    for d, c in near:
        cc = core if c == 0 else other
        if (d, c) != (0, 0):
            pl.semaphore_signal(barrier, inc=1, device_id=(at(z + d, cc), t), device_id_type=MESH)
    for d in (-WIN, WIN, -8, 8):
        pl.semaphore_signal(barrier, inc=1, device_id=(at(z + d, core), t), device_id_type=MESH)
    for k in range(1, NT):
        pl.semaphore_signal(barrier, inc=1, device_id=(dp, t ^ k), device_id_type=MESH)

    copies[0].wait()
    q3[...] = split3(q0[...])
    copies[1].wait()
    left = fold3(dot(q3[...], x[768:1024, :], NT_DIMS))
    copies[5].wait()
    acc = None
    for r in range(3):
        copies[2 + r].wait()
        y = fold3(dot(q3[...], x[256 * r:256 * (r + 1), :], NT_DIMS))
        term = dot(split3(y), act[256 * r:256 * (r + 1), :])
        acc = term if acc is None else acc + term
    p_src[...] = fold3(acc) + left
    pl.semaphore_wait(barrier, len(near) - 1 + 4 + NT - 1)
    for d in (-8, 8):
        pl.semaphore_signal(relay_sem, inc=1, device_id=(at(z + d, core), t), device_id_type=MESH)

    slot = 0
    for d in WINDOW:
        e = -d
        for same in (0, 1):
            if d == 0 and same == 1:
                continue
            cc = core if same else other
            piece = (z + e + NZ) % WIN
            send(p_src.at[tile(piece), pl.ds(pl.multiple_of(cc * LANES, LANES), LANES)],
                 p_rs.at[slot], 0, (at(z + e, cc), t))
            slot += 1
    own = p_src[tile(place), pl.ds(pl.multiple_of(core * LANES, LANES), LANES)]
    wait(recv_sem.at[0], p_rs)
    total = own
    for s in range(2 * WIN - 1):
        total = total + p_rs[s]
    p_far[group] = total
    pl.semaphore_wait(relay_sem, 2)
    for m in FAR_ORDER:
        send(p_far.at[group], p_far.at[group], 1, (at(z + m * WIN, core), t))
    wait(recv_sem.at[1], p_far.at[pl.ds(0, GROUPS - 1)])
    total = p_far[0]
    for m in range(1, GROUPS):
        total = total + p_far[m]
    p_red[...] = total
    rows, cols = tile(place), pl.ds(pl.multiple_of(core * LANES, LANES), LANES)
    p_all[rows, cols] = total
    for d in WINDOW:
        for same in (0, 1):
            if d == 0 and same == 1:
                continue
            send(p_red, p_all.at[rows, cols], 3, (at(z + d, core if same else other), t))
    wait(recv_sem.at[3], p_rs)

    p_sum = p_all[...]

    p3 = split3(p_sum)
    w3[:, 768:1024] = p3
    w3[:, 0:768] = split3(fold3(dot(p3, act[...], NT_DIMS)))

    def compute(b):
        for i in range(b * BATCH, (b + 1) * BATCH):
            j = t ^ ORDER[i]
            v = fold3(dot(w3[...], x[:, pl.ds(pl.multiple_of(j * 256, 256), 256)]))
            q_loc[0, i] = v[:, :LANES]
            q_loc[1, i] = v[:, LANES:]
        part = pl.ds(b * BATCH, BATCH)
        send(q_loc.at[other, part], q_d.at[part], 5, sibling, piece_sem.at[b])

    def forward(b):
        part = pl.ds(b * BATCH, BATCH)
        wait(piece_sem.at[b], q_d.at[part])
        q_s[part] = q_loc[core, part] + q_d[part]
        for i in range(b * BATCH, min((b + 1) * BATCH, NT - 1)):
            send(q_s.at[i], q_x.at[i], 6, (dp, t ^ ORDER[i]))

    def gram_tiles():
        gram = dot(p_sum, jnp.concatenate([p_sum, p_sum], axis=0), NT_DIMS, HIGHEST)
        for i in range(NT):
            g_src[i, 0:4, :] = gram[4 * i:4 * i + 4]
            g_src[i, 4:8, :] = gram[4 * i:4 * i + 4]
        for k in range(1, NT):
            send(g_src.at[t ^ k], g_rs.at[k - 1], 4, (dp, t ^ k))

    batches = NT // BATCH
    for b in range(batches + 1):
        if b < batches:
            compute(b)
        if b > 0:
            forward(b - 1)
        if b == 2:
            gram_tiles()

    wait(recv_sem.at[4], g_rs)
    total = g_src[t]
    for k in range(NT - 1):
        total = total + g_rs[k]
    g_own[...] = total
    g_all[t] = total
    for k in range(1, NT):
        send(g_own, g_all.at[t], 7, (dp, t ^ k))

    wait(recv_sem.at[6], q_x)
    total = q_s[NT - 1]
    for k in range(NT - 1):
        total = total + q_x[k]
    z_src[...] = total

    slot = 0
    for d in WINDOW:
        if d != 0:
            piece = (z - d + NZ) % WIN
            send(z_src.at[tile(piece)], z_rs.at[slot], 8, (at(z - d, core), t))
            slot += 1
    own = z_src[tile(place)]
    wait(recv_sem.at[8], z_rs)
    total = own
    for s in range(WIN - 1):
        total = total + z_rs[s]
    z_far[group] = total
    for m in FAR_ORDER:
        send(z_far.at[group], z_far.at[group], 9, (at(z + m * WIN, core), t))

    wait(recv_sem.at[7], g_rs)
    inverse = invert_factor(jnp.concatenate([g_all[i, 0:4, :] for i in range(NT)], axis=0))
    pb_ref[...] = dot(inverse, p_sum, NN, HIGHEST) * 64.0

    wait(recv_sem.at[9], z_far.at[pl.ds(0, GROUPS - 1)])
    total = z_far[0]
    for m in range(1, GROUPS):
        total = total + z_far[m]
    z_red[...] = total
    z_all[rows, :] = total
    for d in WINDOW:
        if d != 0:
            send(z_red, z_all.at[rows], 10, (at(z + d, core), t))
    wait(recv_sem.at[10], z_rs)

    def columns(tt, cc):
        return pl.ds(pl.multiple_of((tt * 2 + cc) * LANES, LANES), LANES)

    mine = columns(t, core)
    out_ref[:, mine] = dot(inverse, z_all[...], NN, HIGHEST) * (1.0 / 64.0)
    for i in range(NT - 1):
        send(out_ref.at[:, mine], out_ref.at[:, mine], 11, (dp, t ^ ORDER[i]), piece_sem.at[NT + i])
    send(out_ref.at[:, mine], out_ref.at[:, mine], 12, sibling)
    for i in range(NT - 1):
        got = columns(t ^ ORDER[i], core)
        wait(piece_sem.at[NT + i], out_ref.at[:, got])
        send(out_ref.at[:, got], out_ref.at[:, got], 12, sibling)
    wait(recv_sem.at[12], q_d)

    wait(send_sem.at[0], p_rs)
    wait(send_sem.at[1], p_far.at[pl.ds(0, GROUPS - 1)])
    wait(send_sem.at[3], p_rs)
    wait(send_sem.at[4], g_rs)
    wait(send_sem.at[5], q_d)
    wait(send_sem.at[6], q_x)
    wait(send_sem.at[7], g_rs)
    wait(send_sem.at[8], z_rs)
    wait(send_sem.at[9], z_far.at[pl.ds(0, GROUPS - 1)])
    wait(send_sem.at[10], z_rs)
    wait(send_sem.at[11], q_x)
    wait(send_sem.at[12], q_d)


def store(basis, right, basis_hbm, right_hbm, sem):
    copies = [pltpu.make_async_copy(basis, basis_hbm, sem.at[4])]
    for i in range(4):
        rows = pl.ds(i * 16, 16)
        copies.append(pltpu.make_async_copy(right.at[rows], right_hbm.at[rows], sem.at[i]))
    for c in copies:
        c.start()
    for c in copies:
        c.wait()


def local(activations, out_grads, error_memory, q_init):
    any_spec = pl.BlockSpec(memory_space=pl.ANY)
    vmem = pl.BlockSpec(memory_space=pltpu.VMEM)
    piece = (RANK, LANES)
    scratch = [
        pltpu.VMEM((1024, 4096), BF16),
        pltpu.VMEM((768, 256), BF16),
        pltpu.VMEM((RANK, 4096), F32),
        pltpu.VMEM((3 * RANK, 4096), BF16),
        pltpu.VMEM((3 * RANK, 1024), BF16),
        pltpu.VMEM((RANK, 256), F32),
        pltpu.VMEM((2 * WIN - 1, ROWS, LANES), F32),
        pltpu.VMEM((GROUPS, ROWS, LANES), F32),
        pltpu.VMEM((ROWS, LANES), F32),
        pltpu.VMEM((RANK, 256), F32),
        pltpu.VMEM((NT, 8, LANES), F32),
        pltpu.VMEM((NT - 1, 8, LANES), F32),
        pltpu.VMEM((8, LANES), F32),
        pltpu.VMEM((NT, 8, LANES), F32),
        pltpu.VMEM((2, NT) + piece, F32),
        pltpu.VMEM((NT,) + piece, F32),
        pltpu.VMEM((NT,) + piece, F32),
        pltpu.VMEM((NT - 1,) + piece, F32),
        pltpu.VMEM(piece, F32),
        pltpu.VMEM((WIN - 1, ROWS, LANES), F32),
        pltpu.VMEM((GROUPS, ROWS, LANES), F32),
        pltpu.VMEM((ROWS, LANES), F32),
        pltpu.VMEM(piece, F32),
        pltpu.SemaphoreType.DMA((6,)),
        pltpu.SemaphoreType.DMA((14,)),
        pltpu.SemaphoreType.DMA((14,)),
        pltpu.SemaphoreType.DMA((2 * NT,)),
        pltpu.SemaphoreType.REGULAR,
    ]
    basis, right = pl.pallas_call(
        kernel,
        name="powersgd",
        out_shape=(pltpu.VMEM((RANK, 256), F32), pltpu.VMEM((RANK, 4096), F32)),
        in_specs=[any_spec] * 4,
        out_specs=(vmem, vmem),
        scratch_shapes=scratch,
        compiler_params=pltpu.CompilerParams(
            collective_id=0, has_side_effects=True, vmem_limit_bytes=60 * 2**20),
    )(activations, out_grads, error_memory[0], q_init.T)
    basis, right = pl.pallas_call(
        store,
        name="store",
        out_shape=(
            jax.ShapeDtypeStruct((RANK, 256), F32),
            jax.ShapeDtypeStruct((RANK, 4096), F32),
        ),
        in_specs=[any_spec] * 2,
        out_specs=(any_spec, any_spec),
        scratch_shapes=[pltpu.SemaphoreType.DMA((5,))],
        compiler_params=pltpu.CompilerParams(vmem_limit_bytes=2**20),
    )(basis, right)
    return basis.T, right.T


def solution(mesh):
    return jax.shard_map(
        local,
        mesh=mesh,
        in_specs=(P("dp", "tensor"), P("dp", None), P("dp", "tensor", None), P()),
        out_specs=(P("tensor", None), P()),
        check_vma=False,
    )
```

```python
import jax
import jax.numpy as jnp
from jax import lax
from jax.experimental import pallas as pl
from jax.experimental.pallas import tpu as pltpu
from jax.sharding import PartitionSpec as P

MESH = pl.DeviceIdType.MESH
F32 = jnp.float32
BF16 = jnp.bfloat16
HIGHEST = lax.Precision.HIGHEST
NZ = 32
NT = 16
RANK = 64
LANES = 128
WIN = 4
ROWS = RANK // WIN
GROUPS = NZ // WIN
FAR_ORDER = sorted(range(1, GROUPS), key=lambda m: -min(m, GROUPS - m))
WINDOW = sorted(range(-(WIN // 2 - 1), WIN // 2 + 1), key=lambda d: -abs(d))
ORDER = (10, 11, 14, 9, 6, 15, 5, 7, 13, 2, 8, 1, 4, 3, 12, 0)
BATCH = 4
NN = (((1,), (0,)), ((), ()))
NT_DIMS = (((1,), (1,)), ((), ()))


def dot(a, b, dims=NN, precision=None):
    return lax.dot_general(a, b, dims, precision=precision, preferred_element_type=F32)


def split(v):
    high = v.astype(BF16)
    return jnp.concatenate([high, (v - high.astype(F32)).astype(BF16)], axis=0)


def fold(v):
    return v[:RANK] + v[RANK:]


def wait(sem, ref):
    pltpu.make_async_copy(ref, ref, sem).wait()


def invert_factor(gram):
    row = lax.broadcasted_iota(jnp.int32, (RANK, 2 * RANK), 0)
    lane = lax.broadcasted_iota(jnp.int32, (RANK, 2 * RANK), 1)
    m = jnp.where(lane < RANK, gram, jnp.where(lane - RANK == row, 1.0, 0.0))
    scale = jnp.zeros((RANK, 2 * RANK), F32)
    for k in range(RANK):
        col = jnp.broadcast_to(m[:, k:k + 1], m.shape)
        pivot = col[k:k + 1, :]
        scaled = m[k:k + 1, :] / pivot
        scale = jnp.where(row == k, pivot, scale)
        m = m - jnp.where(row > k, col, 0.0) * scaled
    m = m * lax.rsqrt(scale)
    return m[:, RANK:]


def kernel(act_hbm, grd_hbm, err_hbm, q0_hbm, pb_ref, out_ref,
           x, act, q0, q2, w2, p_src, p_rs, p_far, p_red, p_all,
           g_src, g_rs, g_own, g_all,
           q_loc, q_d, q_s, q_x, z_src, z_rs, z_far, z_red, z_all,
           load_sem, send_sem, recv_sem, piece_sem, relay_sem):
    dp = lax.axis_index("dp")
    t = lax.axis_index("tensor")
    z = dp // 2
    core = dp % 2
    other = 1 - core
    sibling = (dp + other - core, t)
    place = z % WIN
    group = z // WIN

    def at(zz, cc):
        return ((zz + NZ) % NZ) * 2 + cc

    def send(src, dst, phase, dev, recv=None):
        pltpu.make_async_remote_copy(
            src_ref=src, dst_ref=dst, send_sem=send_sem.at[phase],
            recv_sem=recv_sem.at[phase] if recv is None else recv,
            device_id=dev, device_id_type=MESH).start()

    def tile(i):
        return pl.ds(pl.multiple_of(i * ROWS, ROWS), ROWS)

    copies = [pltpu.make_async_copy(q0_hbm, q0, load_sem.at[0])]
    copies.append(pltpu.make_async_copy(err_hbm, x.at[pl.ds(768, 256)], load_sem.at[1]))
    for r in range(3):
        copies.append(pltpu.make_async_copy(
            grd_hbm.at[pl.ds(256 * r, 256)], x.at[pl.ds(256 * r, 256)], load_sem.at[2 + r]))
    copies.append(pltpu.make_async_copy(act_hbm, act, load_sem.at[5]))
    for i in (0, 1, 5, 2, 3, 4):
        copies[i].start()

    barrier = pltpu.get_barrier_semaphore()
    near = [(d, c) for d in range(-WIN // 2, WIN // 2 + 1) for c in (0, 1)]
    for d, c in near:
        cc = core if c == 0 else other
        if (d, c) != (0, 0):
            pl.semaphore_signal(barrier, inc=1, device_id=(at(z + d, cc), t), device_id_type=MESH)
    for d in (-WIN, WIN, -8, 8):
        pl.semaphore_signal(barrier, inc=1, device_id=(at(z + d, core), t), device_id_type=MESH)
    for k in range(1, NT):
        pl.semaphore_signal(barrier, inc=1, device_id=(dp, t ^ k), device_id_type=MESH)

    copies[0].wait()
    q2[...] = split(q0[...])
    copies[1].wait()
    left = fold(dot(q2[...], x[768:1024, :], NT_DIMS))
    copies[5].wait()
    acc = None
    for r in range(3):
        copies[2 + r].wait()
        y = fold(dot(q2[...], x[256 * r:256 * (r + 1), :], NT_DIMS))
        term = dot(split(y), act[256 * r:256 * (r + 1), :])
        acc = term if acc is None else acc + term
    p_src[...] = fold(acc) + left
    pl.semaphore_wait(barrier, len(near) - 1 + 4 + NT - 1)
    for d in (-8, 8):
        pl.semaphore_signal(relay_sem, inc=1, device_id=(at(z + d, core), t), device_id_type=MESH)

    slot = 0
    for d in WINDOW:
        e = -d
        for same in (0, 1):
            if d == 0 and same == 1:
                continue
            cc = core if same else other
            piece = (z + e + NZ) % WIN
            send(p_src.at[tile(piece), pl.ds(pl.multiple_of(cc * LANES, LANES), LANES)],
                 p_rs.at[slot], 0, (at(z + e, cc), t))
            slot += 1
    own = p_src[tile(place), pl.ds(pl.multiple_of(core * LANES, LANES), LANES)]
    wait(recv_sem.at[0], p_rs)
    total = own
    for s in range(2 * WIN - 1):
        total = total + p_rs[s]
    p_far[group] = total
    pl.semaphore_wait(relay_sem, 2)
    for m in FAR_ORDER:
        send(p_far.at[group], p_far.at[group], 1, (at(z + m * WIN, core), t))
    wait(recv_sem.at[1], p_far.at[pl.ds(0, GROUPS - 1)])
    total = p_far[0]
    for m in range(1, GROUPS):
        total = total + p_far[m]
    p_red[...] = total
    rows, cols = tile(place), pl.ds(pl.multiple_of(core * LANES, LANES), LANES)
    p_all[rows, cols] = total
    for d in WINDOW:
        for same in (0, 1):
            if d == 0 and same == 1:
                continue
            send(p_red, p_all.at[rows, cols], 3, (at(z + d, core if same else other), t))
    wait(recv_sem.at[3], p_rs)

    p_sum = p_all[...]

    p2 = split(p_sum)
    w2[:, 768:1024] = p2
    w2[:, 0:768] = split(fold(dot(p2, act[...], NT_DIMS)))

    def compute(b):
        for i in range(b * BATCH, (b + 1) * BATCH):
            j = t ^ ORDER[i]
            v = fold(dot(w2[...], x[:, pl.ds(pl.multiple_of(j * 256, 256), 256)]))
            q_loc[0, i] = v[:, :LANES]
            q_loc[1, i] = v[:, LANES:]
        part = pl.ds(b * BATCH, BATCH)
        send(q_loc.at[other, part], q_d.at[part], 5, sibling, piece_sem.at[b])

    def forward(b):
        part = pl.ds(b * BATCH, BATCH)
        wait(piece_sem.at[b], q_d.at[part])
        q_s[part] = q_loc[core, part] + q_d[part]
        for i in range(b * BATCH, min((b + 1) * BATCH, NT - 1)):
            send(q_s.at[i], q_x.at[i], 6, (dp, t ^ ORDER[i]))

    def gram_tiles():
        gram = dot(p_sum, jnp.concatenate([p_sum, p_sum], axis=0), NT_DIMS, HIGHEST)
        for i in range(NT):
            g_src[i, 0:4, :] = gram[4 * i:4 * i + 4]
            g_src[i, 4:8, :] = gram[4 * i:4 * i + 4]
        for k in range(1, NT):
            send(g_src.at[t ^ k], g_rs.at[k - 1], 4, (dp, t ^ k))

    batches = NT // BATCH
    for b in range(batches + 1):
        if b < batches:
            compute(b)
        if b > 0:
            forward(b - 1)
        if b == 2:
            gram_tiles()

    wait(recv_sem.at[4], g_rs)
    total = g_src[t]
    for k in range(NT - 1):
        total = total + g_rs[k]
    g_own[...] = total
    g_all[t] = total
    for k in range(1, NT):
        send(g_own, g_all.at[t], 7, (dp, t ^ k))

    wait(recv_sem.at[6], q_x)
    total = q_s[NT - 1]
    for k in range(NT - 1):
        total = total + q_x[k]
    z_src[...] = total

    slot = 0
    for d in WINDOW:
        if d != 0:
            piece = (z - d + NZ) % WIN
            send(z_src.at[tile(piece)], z_rs.at[slot], 8, (at(z - d, core), t))
            slot += 1
    own = z_src[tile(place)]
    wait(recv_sem.at[8], z_rs)
    total = own
    for s in range(WIN - 1):
        total = total + z_rs[s]
    z_far[group] = total
    for m in FAR_ORDER:
        send(z_far.at[group], z_far.at[group], 9, (at(z + m * WIN, core), t))

    wait(recv_sem.at[7], g_rs)
    inverse = invert_factor(jnp.concatenate([g_all[i, 0:4, :] for i in range(NT)], axis=0))
    pb_ref[...] = dot(inverse, p_sum, NN, HIGHEST) * 64.0

    wait(recv_sem.at[9], z_far.at[pl.ds(0, GROUPS - 1)])
    total = z_far[0]
    for m in range(1, GROUPS):
        total = total + z_far[m]
    z_red[...] = total
    z_all[rows, :] = total
    for d in WINDOW:
        if d != 0:
            send(z_red, z_all.at[rows], 10, (at(z + d, core), t))
    wait(recv_sem.at[10], z_rs)

    def columns(tt, cc):
        return pl.ds(pl.multiple_of((tt * 2 + cc) * LANES, LANES), LANES)

    mine = columns(t, core)
    out_ref[:, mine] = dot(inverse, z_all[...], NN, HIGHEST) * (1.0 / 64.0)
    for i in range(NT - 1):
        send(out_ref.at[:, mine], out_ref.at[:, mine], 11, (dp, t ^ ORDER[i]), piece_sem.at[NT + i])
    send(out_ref.at[:, mine], out_ref.at[:, mine], 12, sibling)
    for i in range(NT - 1):
        got = columns(t ^ ORDER[i], core)
        wait(piece_sem.at[NT + i], out_ref.at[:, got])
        send(out_ref.at[:, got], out_ref.at[:, got], 12, sibling)
    wait(recv_sem.at[12], q_d)

    wait(send_sem.at[0], p_rs)
    wait(send_sem.at[1], p_far.at[pl.ds(0, GROUPS - 1)])
    wait(send_sem.at[3], p_rs)
    wait(send_sem.at[4], g_rs)
    wait(send_sem.at[5], q_d)
    wait(send_sem.at[6], q_x)
    wait(send_sem.at[7], g_rs)
    wait(send_sem.at[8], z_rs)
    wait(send_sem.at[9], z_far.at[pl.ds(0, GROUPS - 1)])
    wait(send_sem.at[10], z_rs)
    wait(send_sem.at[11], q_x)
    wait(send_sem.at[12], q_d)


def store(basis, right, basis_hbm, right_hbm, sem):
    copies = [pltpu.make_async_copy(basis, basis_hbm, sem.at[4])]
    for i in range(4):
        rows = pl.ds(i * 16, 16)
        copies.append(pltpu.make_async_copy(right.at[rows], right_hbm.at[rows], sem.at[i]))
    for c in copies:
        c.start()
    for c in copies:
        c.wait()


def local(activations, out_grads, error_memory, q_init):
    any_spec = pl.BlockSpec(memory_space=pl.ANY)
    vmem = pl.BlockSpec(memory_space=pltpu.VMEM)
    piece = (RANK, LANES)
    scratch = [
        pltpu.VMEM((1024, 4096), BF16),
        pltpu.VMEM((768, 256), BF16),
        pltpu.VMEM((RANK, 4096), F32),
        pltpu.VMEM((2 * RANK, 4096), BF16),
        pltpu.VMEM((2 * RANK, 1024), BF16),
        pltpu.VMEM((RANK, 256), F32),
        pltpu.VMEM((2 * WIN - 1, ROWS, LANES), F32),
        pltpu.VMEM((GROUPS, ROWS, LANES), F32),
        pltpu.VMEM((ROWS, LANES), F32),
        pltpu.VMEM((RANK, 256), F32),
        pltpu.VMEM((NT, 8, LANES), F32),
        pltpu.VMEM((NT - 1, 8, LANES), F32),
        pltpu.VMEM((8, LANES), F32),
        pltpu.VMEM((NT, 8, LANES), F32),
        pltpu.VMEM((2, NT) + piece, F32),
        pltpu.VMEM((NT,) + piece, F32),
        pltpu.VMEM((NT,) + piece, F32),
        pltpu.VMEM((NT - 1,) + piece, F32),
        pltpu.VMEM(piece, F32),
        pltpu.VMEM((WIN - 1, ROWS, LANES), F32),
        pltpu.VMEM((GROUPS, ROWS, LANES), F32),
        pltpu.VMEM((ROWS, LANES), F32),
        pltpu.VMEM(piece, F32),
        pltpu.SemaphoreType.DMA((6,)),
        pltpu.SemaphoreType.DMA((14,)),
        pltpu.SemaphoreType.DMA((14,)),
        pltpu.SemaphoreType.DMA((2 * NT,)),
        pltpu.SemaphoreType.REGULAR,
    ]
    basis, right = pl.pallas_call(
        kernel,
        name="powersgd",
        out_shape=(pltpu.VMEM((RANK, 256), F32), pltpu.VMEM((RANK, 4096), F32)),
        in_specs=[any_spec] * 4,
        out_specs=(vmem, vmem),
        scratch_shapes=scratch,
        compiler_params=pltpu.CompilerParams(
            collective_id=0, has_side_effects=True, vmem_limit_bytes=60 * 2**20),
    )(activations, out_grads, error_memory[0], q_init.T)
    basis, right = pl.pallas_call(
        store,
        name="store",
        out_shape=(
            jax.ShapeDtypeStruct((RANK, 256), F32),
            jax.ShapeDtypeStruct((RANK, 4096), F32),
        ),
        in_specs=[any_spec] * 2,
        out_specs=(any_spec, any_spec),
        scratch_shapes=[pltpu.SemaphoreType.DMA((5,))],
        compiler_params=pltpu.CompilerParams(vmem_limit_bytes=2**20),
    )(basis, right)
    return basis.T, right.T


def solution(mesh):
    return jax.shard_map(
        local,
        mesh=mesh,
        in_specs=(P("dp", "tensor"), P("dp", None), P("dp", "tensor", None), P()),
        out_specs=(P("tensor", None), P()),
        check_vma=False,
    )
```
